256 devices in a mesh: rep: 32 (over x_lo, z, core), tp: 8 (over x_hi, y).
Axes of the slice: x: 4 (x_hi: 2, x_lo: 2; x = x_hi * 2 + x_lo), y: 4, z: 8, core: 2. Of those that a mesh axis runs over, the one named last changes fastest.
Arguments:
- images: bfloat16 [65536, 1024], P(('rep', 'tp')), may hold values from -6 to 6
- labels: int32 [256], P('rep'), may hold values from 0 to 999
- first_weight: bfloat16 [32768, 4096], P('rep', 'tp'), may hold values from -0.1875 to 0.1875
- second_weight: bfloat16 [131072, 1024], P(('rep', 'tp')), may hold values from -0.09375 to 0.09375
- head_weight: bfloat16 [32768, 1000], P('rep', 'tp'), may hold values from -0.1875 to 0.1875
- push_weights: float32 [32], P('rep'), may hold values from 0.5 to 2
- round_index: int32 [1], replicated, may hold values from 0 to 2
- lr_first: float32 [1], replicated, may hold values from 10 to 40
- lr_second: float32 [1], replicated, may hold values from 1 to 4
- lr_head: float32 [1], replicated, may hold values from 0.1 to 0.5
Outputs:
- new_first: bfloat16 [32768, 4096], P('rep', 'tp')
- new_second: bfloat16 [131072, 1024], P(('rep', 'tp'))
- new_head: bfloat16 [32768, 1000], P('rep', 'tp')
- new_mass: float32 [32], P('rep')
The draws below stay inside these ranges and needn't reach their ends.
Inputs may be any that keep to these rules, and one draw needn't show every extreme that they name: `round_index`: k picks the peers at offsets 2^k and 2^(k+1) among the 32 replicas.
All inputs are finite; a program needn't handle non-finite values.
Results may differ from the reference program's by a relative error of at most 0.0056.
The reference program's roundings to bfloat16 on the way (of `normed` and `dpre`) count: a program that leaves them out, or rounds other values in their place, can miss the bound.
Values may be sent and summed in bfloat16 or wider, within the bound.
No kernel may reach another device: no remote copies, remote signals or barrier semaphores. Data moves between devices by JAX's collectives and lax.ppermute only.
A program may use at most 64 MiB of HBM per device.

```python
import math
from functools import partial
import jax
import jax.numpy as jnp
from jax import lax

D = 1024
FF = 4096
CLASSES = 1000
SEQ = 256
IMG = 8
N_REP = 32


def touch_ends(values, stream_key, smallest, top_value):
    longest = values.shape.index(max(values.shape))
    spots = []
    for shift in (0, 1):
        where = [jax.random.randint(jax.random.fold_in(stream_key, axis), (), 0, length) for axis, length in enumerate(values.shape)]
        where[longest] = (where[longest] + shift) % values.shape[longest]
        spots.append(tuple(where))
    return values.at[spots[0]].set(smallest).at[spots[1]].set(top_value)


def shard_levels(own_key, dims, pieces, low, high):
    loudness = 1.0
    for axis_at, shards_of in pieces:
        steps = jax.random.uniform(jax.random.fold_in(jax.random.fold_in(own_key, 6), axis_at), (shards_of,), jnp.float32, low / len(pieces), high / len(pieces))
        loudness = loudness * jnp.repeat(jnp.exp(steps), dims[axis_at] // shards_of).reshape((-1,) + (1,) * (len(dims) - 1 - axis_at))
    return loudness


def scatter_about(key, extent, width, limit, cuts=(), kind=jnp.bfloat16):
    factor_of = shard_levels(key, extent, cuts, -0.22, 0.18) if cuts else 1.0
    values = jax.random.normal(key, extent, jnp.float32) * width * factor_of
    return jnp.minimum(jnp.maximum(values, -limit), limit).astype(kind)


def setup_inputs(seed: int = 0) -> dict:
    seeds = jax.random.split(jax.random.key(seed), 11)
    images = scatter_about(seeds[0], (N_REP * IMG * SEQ, D), 1.0, 6.0, ((0, 256),))
    labels = touch_ends(jax.random.randint(seeds[1], (N_REP * IMG,), 0, CLASSES), jax.random.fold_in(seeds[1], 1), 0, CLASSES - 1).astype(jnp.int32)
    first_weight = scatter_about(seeds[2], (N_REP * D, FF), D ** -0.5, 0.1875, ((0, 32), (1, 8)))
    second_weight = scatter_about(seeds[3], (N_REP * FF, D), FF ** -0.5, 0.09375, ((0, 256),))
    head_weight = scatter_about(seeds[4], (N_REP * D, CLASSES), D ** -0.5, 0.1875, ((0, 32), (1, 8)))
    push_weights = jnp.clip(jnp.exp(math.log(2.0) - 1.3862944 * jax.random.uniform(seeds[5], (N_REP,), jnp.float32) ** shard_levels(seeds[5], (N_REP,), ((0, 32),), -0.2, 0.2)), 0.5, 2.0)
    round_index = jax.random.randint(seeds[6], (1,), 0, 3).astype(jnp.int32)
    lr_first = jnp.clip(jnp.exp(jax.random.uniform(seeds[7], (1,), jnp.float32, math.log(10.0), math.log(40.0))), 10.0, 40.0)
    lr_second = jnp.clip(jnp.exp(jax.random.uniform(seeds[8], (1,), jnp.float32, math.log(1.0), math.log(4.0))), 1.0, 4.0)
    lr_head = jnp.clip(jnp.exp(jax.random.uniform(seeds[9], (1,), jnp.float32, math.log(0.1), math.log(0.5))), 0.1, 0.5)
    return {"images": images, "labels": labels, "first_weight": first_weight, "second_weight": second_weight, "head_weight": head_weight, "push_weights": push_weights, "round_index": round_index, "lr_first": lr_first, "lr_second": lr_second, "lr_head": lr_head}


COEF = 0.7978845608
CUBIC = 0.044715
HIGH = lax.Precision.HIGHEST

def normalize(rows):
    values = rows.astype(jnp.float32)
    center = values - lax.optimization_barrier(jnp.mean(values, axis=-1, keepdims=True))
    spread = lax.optimization_barrier(jnp.mean(center * center, axis=-1, keepdims=True))
    return (center * lax.rsqrt(spread + 1e-05)).astype(jnp.bfloat16)

def gelu_pair(pre):
    tanh_val = jnp.tanh(COEF * (pre + CUBIC * pre * pre * pre))
    value = 0.5 * pre * (1.0 + tanh_val)
    slope = 0.5 * (1.0 + tanh_val) + 0.5 * pre * (1.0 - tanh_val * tanh_val) * COEF * (1.0 + 3.0 * CUBIC * pre * pre)
    return (value, slope)

def replica_step(packed, lr_first, lr_second, lr_head):
    tokens, classes, first, second, head, mass = packed
    z_first = (first.astype(jnp.float32) / mass).astype(jnp.bfloat16)
    z_second = (second.astype(jnp.float32) / mass).astype(jnp.bfloat16)
    z_head = (head.astype(jnp.float32) / mass).astype(jnp.bfloat16)
    normed = normalize(tokens)
    pre = jnp.dot(normed, z_first, preferred_element_type=jnp.float32)
    act, slope = gelu_pair(pre)
    mean_act = lax.optimization_barrier(jnp.mean(act.reshape(IMG, SEQ, FF), axis=1))
    mean_tok = lax.optimization_barrier(jnp.mean(tokens.astype(jnp.float32).reshape(IMG, SEQ, D), axis=1))
    second_f = z_second.astype(jnp.float32)
    pooled = mean_tok + jnp.dot(mean_act, second_f, precision=HIGH)
    pooled_b = pooled.astype(jnp.bfloat16)
    logits = jnp.dot(pooled_b, z_head, preferred_element_type=jnp.float32)
    expo = jnp.exp(logits)
    prob = expo / lax.optimization_barrier(jnp.sum(expo, axis=1, keepdims=True))
    onehot = (classes[:, None] == jnp.arange(CLASSES, dtype=jnp.int32)[None, :]).astype(jnp.float32)
    dlog = (prob - onehot) / IMG
    grad_head = jnp.dot(pooled_b.astype(jnp.float32).T, dlog, precision=HIGH)
    dpool = jnp.dot(dlog, z_head.astype(jnp.float32).T, precision=HIGH)
    dmean = jnp.dot(dpool, second_f.T, precision=HIGH)
    grad_second = jnp.dot(mean_act.T, dpool, precision=HIGH)
    dpre = (dmean[:, None, :] / SEQ * slope.reshape(IMG, SEQ, FF)).reshape(IMG * SEQ, FF).astype(jnp.bfloat16)
    grad_first = jnp.dot(normed.T, dpre, preferred_element_type=jnp.float32)
    sent_first = (first.astype(jnp.float32) - lr_first * grad_first).astype(jnp.bfloat16)
    sent_second = (second.astype(jnp.float32) - lr_second * grad_second).astype(jnp.bfloat16)
    sent_head = (head.astype(jnp.float32) - lr_head * grad_head).astype(jnp.bfloat16)
    sent_mass = mass.astype(jnp.bfloat16)
    return (sent_first, sent_second, sent_head, sent_mass)

def reference(images, labels, first_weight, second_weight, head_weight, push_weights, round_index, lr_first, lr_second, lr_head):
    packed = (images.reshape(N_REP, IMG * SEQ, D), labels.reshape(N_REP, IMG), first_weight.reshape(N_REP, D, FF), second_weight.reshape(N_REP, FF, D), head_weight.reshape(N_REP, D, CLASSES), push_weights)
    step_fn = partial(replica_step, lr_first=lr_first[0], lr_second=lr_second[0], lr_head=lr_head[0])
    sent_first, sent_second, sent_head, sent_mass = lax.map(step_fn, packed)
    near_off = jnp.left_shift(jnp.int32(1), round_index[0])
    far_off = near_off * 2

    def spread(stack):
        values = stack.astype(jnp.float32)
        return (values + jnp.roll(values, near_off, axis=0) + jnp.roll(values, far_off, axis=0)) / 3.0
    new_first = spread(sent_first).astype(jnp.bfloat16).reshape(N_REP * D, FF)
    new_second = spread(sent_second).astype(jnp.bfloat16).reshape(N_REP * FF, D)
    new_head = spread(sent_head).astype(jnp.bfloat16).reshape(N_REP * D, CLASSES)
    new_mass = spread(sent_mass)
    return (new_first, new_second, new_head, new_mass)
```

```python
from functools import partial

import jax
import jax.numpy as jnp
from jax import lax
from jax.experimental import pallas as pl
from jax.experimental.pallas import tpu as pltpu
from jax.sharding import PartitionSpec as P

SEQ = 256
IMG = 8
D = 1024

COEF = 0.7978845608
CUBIC = 0.044715
F32 = jnp.float32
BF16 = jnp.bfloat16

VMEM = pl.BlockSpec(memory_space=pltpu.VMEM)
SMEM = pl.BlockSpec(memory_space=pltpu.SMEM)
PARAMS = pltpu.CompilerParams(vmem_limit_bytes=40 * 1024 * 1024)


def call(body, out_shapes, n_in, scalars=(), scratch=()):
    specs = [SMEM if i in scalars else VMEM for i in range(n_in)]
    single = not isinstance(out_shapes, (list, tuple))
    return pl.pallas_call(
        body,
        out_shape=out_shapes,
        in_specs=specs,
        out_specs=VMEM if single else [VMEM] * len(out_shapes),
        scratch_shapes=list(scratch),
        compiler_params=PARAMS,
    )


def split3(v):
    a = v.astype(BF16)
    r = v - a.astype(F32)
    b = r.astype(BF16)
    c = (r - b.astype(F32)).astype(BF16)
    return a, b, c


def dot(a, b, dims):
    return lax.dot_general(a, b, (dims, ((), ())), preferred_element_type=F32)


def exact_right(a, b, dims):
    n = a.shape[0]
    p = dot(jnp.concatenate(split3(a), axis=0), b, dims)
    return p[:n] + p[n : 2 * n] + p[2 * n : 3 * n]


def outer(a, b):
    a1, a2, a3 = split3(a)
    b1, b2, b3 = split3(b)
    left = jnp.concatenate([a1, a1, a1, a2, a2, a3], axis=0)
    right = jnp.concatenate([b1, b2, b3, b1, b2, b1], axis=0)
    return dot(left, right, ((0,), (0,)))


def norm_kernel(x_ref, o_ref, m_ref):
    rows = x_ref.shape[0]
    step = 64
    total = jnp.zeros((1, D), F32)
    for at in range(0, rows, step):
        v = x_ref[at : at + step, :].astype(F32)
        total = total + jnp.sum(v, axis=0, keepdims=True)
        center = v - jnp.mean(v, axis=-1, keepdims=True)
        spread = jnp.mean(center * center, axis=-1, keepdims=True)
        o_ref[at : at + step, :] = (center * lax.rsqrt(spread + 1e-05)).astype(BF16)
    m_ref[...] = total / SEQ


def scale_kernel(mass_ref, w_ref, o_ref):
    o_ref[...] = (w_ref[...].astype(F32) / mass_ref[0]).astype(BF16)


def forward_kernel(x_ref, z_ref, sum_ref, slope_ref, pre_ref):
    rows = x_ref.shape[0]
    pre_ref[...] = dot(x_ref[...], z_ref[...], ((1,), (0,)))
    step = 32
    total = jnp.zeros((8, z_ref.shape[1]), F32)
    for at in range(0, rows, step):
        pre = pre_ref[at : at + step, :]
        square = pre * pre
        t = jnp.tanh(COEF * (pre + CUBIC * square * pre))
        act = 0.5 * pre * (1.0 + t)
        slope_ref[at : at + step, :] = 0.5 * (1.0 + t) + 0.5 * pre * (1.0 - t * t) * COEF * (
            1.0 + 3.0 * CUBIC * square
        )
        total = total + jnp.sum(act.reshape(step // 8, 8, act.shape[1]), axis=0)
    sum_ref[...] = jnp.sum(total, axis=0, keepdims=True)


def rows_of(index, rows, width):
    at = lax.broadcasted_iota(jnp.int32, (IMG, width), 0)
    return jnp.where(at == index, jnp.broadcast_to(rows, (IMG, width)), 0.0)


def pool_kernel(n_sums, slots, *refs):
    order_ref = refs[0]
    sums = refs[1 : 1 + n_sums]
    z_ref, tok_ref, act_ref, out_ref = refs[1 + n_sums :]
    hidden = z_ref.shape[0]
    mean_act = jnp.zeros((IMG, hidden), F32)
    for ref, slot in zip(sums, slots):
        mean_act = mean_act + rows_of(order_ref[slot], ref[...], hidden)
    mean_act = mean_act / SEQ
    act_ref[...] = mean_act
    part = exact_right(mean_act, z_ref[...], ((1,), (0,))) + rows_of(order_ref[0], tok_ref[...], D)
    out_ref[...] = jnp.broadcast_to(part[None], out_ref.shape)


def logit_kernel(parts_ref, zh_ref, pooled_ref, expo_ref, out_ref):
    pooled = parts_ref[0]
    for i in range(1, parts_ref.shape[0]):
        pooled = pooled + parts_ref[i]
    pooled_b = pooled.astype(BF16)
    pooled_ref[...] = pooled_b.astype(F32)
    zh = zh_ref[...]
    expo = jnp.exp(dot(pooled_b, zh, ((1,), (0,))))
    expo_ref[...] = expo
    part = exact_right(expo, zh, ((1,), (1,)))
    total = jnp.broadcast_to(jnp.sum(expo, axis=1, keepdims=True), (IMG, 128))
    out_ref[...] = jnp.broadcast_to(jnp.concatenate([part, total], axis=1)[None], out_ref.shape)


def grad_kernel(parts_ref, hot_ref, own_hot_ref, expo_ref, z_ref, act_ref, pooled_ref, mass_ref, dmean_ref, pack_ref):
    both = parts_ref[0]
    for i in range(1, parts_ref.shape[0]):
        both = both + parts_ref[i]
    hot = hot_ref[0].astype(F32)
    for i in range(1, hot_ref.shape[0]):
        hot = hot + hot_ref[i].astype(F32)
    total = both[:, D : D + 1]
    dpool = (both[:, :D] / total - hot) / IMG
    dlog = (expo_ref[...] / total - own_hot_ref[...]) / IMG
    dmean_ref[...] = exact_right(dpool, z_ref[...], ((1,), (1,)))
    hidden = z_ref.shape[0]
    classes = dlog.shape[1]
    pack_ref[:, :hidden] = act_ref[...]
    pack_ref[:, hidden : hidden + D] = dpool
    pack_ref[:, hidden + D : hidden + 2 * D] = pooled_ref[...]
    pack_ref[:, hidden + 2 * D :] = jnp.full((IMG, 128), mass_ref[0], F32)
    pack_ref[:, hidden + 2 * D : hidden + 2 * D + classes] = dlog


def first_kernel(slots, *refs):
    n = len(slots)
    order_ref, lr_ref = refs[0], refs[1]
    xs, slopes = refs[2 : 2 + n], refs[2 + n : 2 + 2 * n]
    dmean_ref, w_ref, o_ref = refs[2 + 2 * n : 5 + 2 * n]
    dpre_refs = refs[5 + 2 * n :]
    dmean = dmean_ref[...] / SEQ
    hidden = dmean.shape[1]
    for slope_ref, dpre_ref, slot in zip(slopes, dpre_refs, slots):
        at = lax.broadcasted_iota(jnp.int32, (IMG, hidden), 0)
        row = jnp.sum(jnp.where(at == order_ref[slot], dmean, 0.0), axis=0, keepdims=True)
        for lo in range(0, slope_ref.shape[0], 32):
            dpre_ref[lo : lo + 32, :] = (row * slope_ref[lo : lo + 32, :]).astype(BF16)
    width = 256
    for lo in range(0, D, width):
        grad = jnp.zeros((width, hidden), F32)
        for x_ref, dpre_ref in zip(xs, dpre_refs):
            grad = grad + dot(x_ref[:, lo : lo + width], dpre_ref[...], ((0,), (0,)))
        o_ref[lo : lo + width, :] = (
            w_ref[lo : lo + width, :].astype(F32) - lr_ref[0] * grad
        ).astype(BF16)


def rest_kernel(lr2_ref, lrh_ref, *refs):
    packs, seconds, heads = refs[0:3], refs[3:6], refs[6:9]
    o2_ref, oh_ref = refs[9:11]
    hidden = seconds[0].shape[0]
    classes = heads[0].shape[1]
    total = None
    for pack, w in zip(packs, seconds):
        grad = outer(pack[:, :hidden], pack[:, hidden : hidden + D])
        sent = (w[...].astype(F32) - lr2_ref[0] * grad).astype(BF16).astype(F32)
        total = sent if total is None else total + sent
    o2_ref[...] = (total / 3.0).astype(BF16)
    total = None
    for pack, w in zip(packs, heads):
        left = pack[:, hidden + D : hidden + 2 * D].astype(BF16)
        right = pack[:, hidden + 2 * D : hidden + 2 * D + classes]
        grad = dot(jnp.concatenate([left] * 3, axis=0), jnp.concatenate(split3(right), axis=0), ((0,), (0,)))
        sent = (w[...].astype(F32) - lrh_ref[0] * grad).astype(BF16).astype(F32)
        total = sent if total is None else total + sent
    oh_ref[...] = (total / 3.0).astype(BF16)


def mean_kernel(a_ref, b_ref, c_ref, o_ref):
    step = 128
    for at in range(0, a_ref.shape[0], step):
        s = slice(at, at + step)
        o_ref[s, :] = (
            (a_ref[s, :].astype(F32) + b_ref[s, :].astype(F32) + c_ref[s, :].astype(F32)) / 3.0
        ).astype(BF16)


def tp_move(value, by_x, by_y):
    pairs = [(x * 4 + y, (x + by_x) % 2 * 4 + (y + by_y) % 4) for x in range(2) for y in range(4)]
    return lax.ppermute(value, "tp", pairs)


def rep_move(value, by):
    return lax.ppermute(value, "rep", [(i, (i + by) % 32) for i in range(32)])


def to_all(copies):
    return lax.all_to_all(copies, "tp", 0, 0, tiled=True)


def body(
    near,
    images,
    labels,
    first_weight,
    second_weight,
    head_weight,
    push_weights,
    lr_first,
    lr_second,
    lr_head,
):
    hidden = first_weight.shape[1]
    classes = head_weight.shape[1]
    t = lax.axis_index("tp")
    tx, ty = t // 4, t % 4

    second_near = rep_move(second_weight, near)
    head_near = rep_move(head_weight, near)
    second_far = rep_move(second_near, near)
    head_far = rep_move(head_near, near)

    shape = jax.ShapeDtypeStruct
    own, tok = call(norm_kernel, [shape((SEQ, D), BF16), shape((1, D), F32)], 1)(images)

    def ring(block):
        up = tp_move(block, 0, 1)
        down = tp_move(block, 0, -1)
        half = SEQ // 2
        over_a = tp_move(up[:half], 0, 1)
        over_b = tp_move(down[half:], 0, -1)
        return [up, down, over_a, over_b]

    across = tp_move(own, 1, 0)
    blocks = [own, across] + ring(own) + ring(across)
    slots = [0, 4, 3, 1, 2, 2, 7, 5, 6, 6]
    order = jnp.stack([(tx + j // 4) % 2 * 4 + (ty + j % 4) % 4 for j in range(8)]).astype(jnp.int32)

    def scaled(w):
        return call(scale_kernel, shape(w.shape, BF16), 2, (0,))(push_weights, w)

    z_first, z_second, z_head = scaled(first_weight), scaled(second_weight), scaled(head_weight)
    class_ids = t * classes + jnp.arange(classes, dtype=jnp.int32)
    onehot = (labels[:, None] == class_ids[None, :]).astype(F32)
    hot_part = lax.dot_general(
        onehot.astype(BF16), z_head, (((1,), (1,)), ((), ())), preferred_element_type=F32
    ).astype(BF16)
    hot = to_all(jnp.broadcast_to(hot_part[None], (8, IMG, D)))

    sums, slopes = [], []
    for block in blocks:
        rows = block.shape[0]
        s, slope = call(
            forward_kernel,
            [shape((1, hidden), F32), shape((rows, hidden), F32)],
            2,
            (),
            [pltpu.VMEM((rows, hidden), F32)],
        )(block, z_first)
        sums.append(s)
        slopes.append(slope)

    mean_act, part = call(
        partial(pool_kernel, len(sums), slots),
        [shape((IMG, hidden), F32), shape((8, IMG, D), F32)],
        3 + len(sums),
        (0,),
    )(order, *sums, z_second, tok)
    pooled, expo, part = call(
        logit_kernel,
        [shape((IMG, D), F32), shape((IMG, classes), F32), shape((8, IMG, D + 128), F32)],
        2,
    )(to_all(part), z_head)
    mass = push_weights.astype(BF16).astype(F32)
    dmean, pack = call(
        grad_kernel,
        [shape((IMG, hidden), F32), shape((IMG, hidden + 2 * D + 128), F32)],
        8,
        (7,),
    )(to_all(part), hot, onehot, expo, z_second, mean_act, pooled, mass)
    pack_near = rep_move(pack, near)
    pack_far = rep_move(pack_near, near)

    n = len(blocks)
    sent = call(
        partial(first_kernel, slots),
        shape(first_weight.shape, BF16),
        4 + 2 * n,
        (0, 1),
        [pltpu.VMEM((b.shape[0], hidden), BF16) for b in blocks],
    )(order, lr_first, *blocks, *slopes, dmean, first_weight)
    sent_near = rep_move(sent, near)
    sent_far = rep_move(sent_near, near)

    new_second, new_head = call(
        rest_kernel,
        [shape(second_weight.shape, BF16), shape(head_weight.shape, BF16)],
        11,
        (0, 1),
    )(
        lr_second,
        lr_head,
        pack,
        pack_near,
        pack_far,
        second_weight,
        second_near,
        second_far,
        head_weight,
        head_near,
        head_far,
    )
    new_first = call(mean_kernel, shape(first_weight.shape, BF16), 3)(sent, sent_near, sent_far)
    new_mass = (mass + pack_near[0, -1:] + pack_far[0, -1:]) / 3.0
    return new_first, new_second, new_head, new_mass


def local(images, labels, first_weight, second_weight, head_weight, push_weights, round_index, *rates):
    level = jnp.clip(round_index[0], 0, 2)
    return lax.switch(
        level,
        [partial(body, 1 << step) for step in range(3)],
        images,
        labels,
        first_weight,
        second_weight,
        head_weight,
        push_weights,
        *rates,
    )


def solution(mesh):
    return jax.shard_map(
        local,
        mesh=mesh,
        in_specs=(
            P(("rep", "tp"), None),
            P("rep"),
            P("rep", "tp"),
            P(("rep", "tp"), None),
            P("rep", "tp"),
            P("rep"),
            P(),
            P(),
            P(),
            P(),
        ),
        out_specs=(P("rep", "tp"), P(("rep", "tp"), None), P("rep", "tp"), P("rep")),
        check_vma=False,
    )
```

```python
from functools import partial

import jax
import jax.numpy as jnp
from jax import lax
from jax.experimental import pallas as pl
from jax.experimental.pallas import tpu as pltpu
from jax.sharding import PartitionSpec as P

SEQ = 256
IMG = 8
D = 1024

COEF = 0.7978845608
CUBIC = 0.044715
F32 = jnp.float32
BF16 = jnp.bfloat16

VMEM = pl.BlockSpec(memory_space=pltpu.VMEM)
SMEM = pl.BlockSpec(memory_space=pltpu.SMEM)
ANY = pl.BlockSpec(memory_space=pl.ANY)
PARAMS = pltpu.CompilerParams(vmem_limit_bytes=10 * 1024 * 1024)


def call(body, out_shapes, n_in, scalars=(), scratch=(), flops=0, size=0):
    specs = [SMEM if i in scalars else VMEM for i in range(n_in)]
    single = not isinstance(out_shapes, (list, tuple))
    return pl.pallas_call(
        body,
        out_shape=out_shapes,
        in_specs=specs,
        out_specs=VMEM if single else [VMEM] * len(out_shapes),
        scratch_shapes=list(scratch),
        compiler_params=PARAMS,
        cost_estimate=pl.CostEstimate(flops=flops, bytes_accessed=size, transcendentals=0),
    )


def split3(v):
    a = v.astype(BF16)
    r = v - a.astype(F32)
    b = r.astype(BF16)
    c = (r - b.astype(F32)).astype(BF16)
    return a, b, c


def dot(a, b, dims):
    return lax.dot_general(a, b, (dims, ((), ())), preferred_element_type=F32)


def exact_right(a, b, dims):
    n = a.shape[0]
    p = dot(jnp.concatenate(split3(a), axis=0), b, dims)
    return p[:n] + p[n : 2 * n] + p[2 * n : 3 * n]


def outer(a, b):
    a1, a2, a3 = split3(a)
    b1, b2, b3 = split3(b)
    left = jnp.concatenate([a1, a1, a1, a2, a2, a3], axis=0)
    right = jnp.concatenate([b1, b2, b3, b1, b2, b1], axis=0)
    return dot(left, right, ((0,), (0,)))


def norm_kernel(x_ref, o_ref, m_ref):
    rows = x_ref.shape[0]
    step = 64
    total = jnp.zeros((1, D), F32)
    for at in range(0, rows, step):
        v = x_ref[at : at + step, :].astype(F32)
        total = total + jnp.sum(v, axis=0, keepdims=True)
        center = v - jnp.mean(v, axis=-1, keepdims=True)
        spread = jnp.mean(center * center, axis=-1, keepdims=True)
        o_ref[at : at + step, :] = (center * lax.rsqrt(spread + 1e-05)).astype(BF16)
    m_ref[...] = total / SEQ


def stack_kernel(second_ref, head_ref, o_ref):
    rows = second_ref.shape[0]
    o_ref[:rows, :] = second_ref[...]
    classes = head_ref.shape[1]
    width = 256
    for at in range(0, D, width):
        part = head_ref[at : at + width, :].astype(F32)
        part = jnp.concatenate([part, jnp.zeros((width, 128 - classes), F32)], axis=1)
        o_ref[rows:, at : at + width] = part.T.astype(BF16)


def gather_kernel(picks, n, *refs):
    for pick, o_ref in zip(picks, refs[n:]):
        to = 0
        for which, begin, rows in pick:
            o_ref[to : to + rows, :] = refs[which][begin : begin + rows, :]
            to += rows


def gathered(picks, *arrays):
    shapes = [jax.ShapeDtypeStruct((sum(p[2] for p in pick), arrays[0].shape[1]), BF16) for pick in picks]
    return call(partial(gather_kernel, picks, len(arrays)), shapes, len(arrays), size=2000000)(*arrays)


def scale_kernel(mass_ref, w_ref, o_ref):
    step = 128

    def slab(i, carry):
        at = pl.ds(pl.multiple_of(i * step, step), step)
        o_ref[at, :] = (w_ref[at, :].astype(F32) / mass_ref[0]).astype(BF16)
        return carry

    lax.fori_loop(0, w_ref.shape[0] // step, slab, 0)


def rows_of(index, rows, width):
    at = lax.broadcasted_iota(jnp.int32, (IMG, width), 0)
    return jnp.where(at == index, jnp.broadcast_to(rows, (IMG, width)), 0.0)


def forward_kernel(
    pieces, order_ref, x_ref, z_ref, act_in, act_ref, slope_out, pre_ref, slope_ref, sems
):
    step = 32
    part = 128
    width = z_ref.shape[1]
    act_sum = act_in[...]
    copies = []
    to = 0
    for begin, rows, slot in pieces:
        pre_ref[:rows, :] = dot(x_ref[begin : begin + rows, :], z_ref[...], ((1,), (0,)))
        total = jnp.zeros((8, width), F32)
        for at in range(0, rows, step):
            pre = pre_ref[at : at + step, :]
            square = pre * pre
            t = jnp.tanh(COEF * (pre + CUBIC * square * pre))
            act = 0.5 * pre * (1.0 + t)
            slope_ref[to : to + step, :] = 0.5 * (1.0 + t) + 0.5 * pre * (1.0 - t * t) * COEF * (
                1.0 + 3.0 * CUBIC * square
            )
            total = total + jnp.sum(act.reshape(step // 8, 8, width), axis=0)
            to += step
            if to % part == 0:
                where = pl.ds(to - part, part)
                copies.append(
                    pltpu.make_async_copy(slope_ref.at[where], slope_out.at[where], sems.at[to // part - 1])
                )
                copies[-1].start()
        act_sum = act_sum + rows_of(order_ref[slot], jnp.sum(total, axis=0, keepdims=True), width)
    act_ref[...] = act_sum
    for copy in copies:
        copy.wait()


def pool_kernel(order_ref, sum_ref, z_ref, tok_ref, hot_ref, act_ref, out_ref):
    mean_act = sum_ref[...] / SEQ
    act_ref[...] = mean_act
    part = exact_right(mean_act, z_ref[...], ((1,), (0,))) + rows_of(order_ref[0], tok_ref[...], D)
    out_ref[:, :D] = part
    out_ref[:, D:] = hot_ref[...]


def add_kernel(own_ref, over_ref, up_ref, down_ref, o_ref):
    o_ref[...] = (own_ref[...] + over_ref[...]) + (up_ref[...] + down_ref[...])


def pair_kernel(one_ref, two_ref, o_ref):
    o_ref[...] = one_ref[...] + two_ref[...]


def logit_kernel(own_ref, over_ref, up_ref, down_ref, zh_ref, pooled_ref, hot_ref, expo_ref, out_ref):
    both = (own_ref[...] + over_ref[...]) + (up_ref[...] + down_ref[...])
    pooled = both[:, :D]
    hot_ref[...] = both[:, D:]
    pooled_b = pooled.astype(BF16)
    pooled_ref[...] = pooled_b.astype(F32)
    zh = zh_ref[...]
    expo = jnp.exp(dot(pooled_b, zh, ((1,), (0,))))
    expo_ref[...] = expo
    part = exact_right(expo, zh, ((1,), (1,)))
    total = jnp.broadcast_to(jnp.sum(expo, axis=1, keepdims=True), (IMG, 128))
    out_ref[:, :D] = part
    out_ref[:, D:] = total


def grad_kernel(one_ref, two_ref, hot_ref, own_hot_ref, expo_ref, z_ref, act_ref, pooled_ref, mass_ref, dmean_ref, pack_ref):
    both = one_ref[...] + two_ref[...]
    total = both[:, D : D + 1]
    dpool = (both[:, :D] / total - hot_ref[...]) / IMG
    dlog = (expo_ref[...] / total - own_hot_ref[...]) / IMG
    dmean_ref[...] = exact_right(dpool, z_ref[...], ((1,), (1,)))
    hidden = z_ref.shape[0]
    classes = dlog.shape[1]
    pack_ref[:, :hidden] = act_ref[...]
    pack_ref[:, hidden : hidden + D] = dpool
    pack_ref[:, hidden + D : hidden + 2 * D] = pooled_ref[...]
    pack_ref[:, hidden + 2 * D :] = jnp.full((IMG, 128), mass_ref[0], F32)
    pack_ref[:, hidden + 2 * D : hidden + 2 * D + classes] = dlog


def dpre_kernel(layout, order_ref, *refs):
    n = len(layout)
    slopes, dmean_ref, outs = refs[:n], refs[n], refs[n + 1 : 2 * n + 1]
    held, sems = refs[2 * n + 1 :]
    copies = []
    to = 0
    for i, ref in enumerate(slopes):
        copies.append(pltpu.make_async_copy(ref, held.at[pl.ds(to, ref.shape[0])], sems.at[i]))
        copies[-1].start()
        to += ref.shape[0]
    dmean = dmean_ref[...] / SEQ
    hidden = dmean.shape[1]
    step = 32
    base = 0
    for pieces, copy, dpre_ref in zip(layout, copies, outs):
        copy.wait()
        to = 0
        for _, rows, slot in pieces:
            at = lax.broadcasted_iota(jnp.int32, (IMG, hidden), 0)
            row = jnp.sum(jnp.where(at == order_ref[slot], dmean, 0.0), axis=0, keepdims=True)
            for _ in range(0, rows, step):
                dpre_ref[to : to + step, :] = (row * held[base + to : base + to + step, :]).astype(BF16)
                to += step
        base += to


def first_kernel(layout, begin, lr_ref, *refs):
    n = len(layout)
    xs, dpre_refs = refs[:n], refs[n : 2 * n]
    w_ref, o_ref = refs[2 * n :]
    hidden = o_ref.shape[1]
    width = 128
    for lo in range(0, o_ref.shape[0], width):
        at = begin + lo
        grad = jnp.zeros((width, hidden), F32)
        for pieces, x_ref, dpre_ref in zip(layout, xs, dpre_refs):
            to = 0
            for row, rows, _ in pieces:
                grad = grad + dot(
                    x_ref[row : row + rows, at : at + width], dpre_ref[to : to + rows, :], ((0,), (0,))
                )
                to += rows
        o_ref[lo : lo + width, :] = (
            w_ref[at : at + width, :].astype(F32) - lr_ref[0] * grad
        ).astype(BF16)


def rest_kernel(bounds, lr2_ref, lrh_ref, *refs):
    n = len(bounds) - 1
    packs, own_ref, near_ref, fars = refs[0:3], refs[3], refs[4], refs[5 : 5 + n]
    o2_ref, oh_ref = refs[5 + n :]
    hidden = o2_ref.shape[0]
    classes = oh_ref.shape[1]
    width = 128

    def mean(rate, grads, weights):
        total = None
        for grad, w in zip(grads, weights):
            sent = (w.astype(F32) - rate * grad).astype(BF16).astype(F32)
            total = sent if total is None else total + sent
        return (total / 3.0).astype(BF16)

    for i in range(n):

        def block(j, carry, i=i):
            lo = pl.ds(pl.multiple_of(j * width, width), width)
            at = pl.ds(pl.multiple_of(bounds[i] + j * width, width), width)
            grads = [outer(pack[:, at], pack[:, hidden : hidden + D]) for pack in packs]
            o2_ref[at, :] = mean(lr2_ref[0], grads, (own_ref[at, :], near_ref[at, :], fars[i][lo, :]))
            return carry

        lax.fori_loop(0, (min(bounds[i + 1], hidden) - bounds[i]) // width, block, 0)
    grads = []
    for pack in packs:
        left = jnp.concatenate(split3(pack[:, hidden + 2 * D :]), axis=0)
        right = pack[:, hidden + D : hidden + 2 * D].astype(BF16)
        grads.append(dot(left, jnp.concatenate([right] * 3, axis=0), ((0,), (0,))))
    last = fars[n - 1].shape[0] - width
    new = mean(lrh_ref[0], grads, (own_ref[hidden:, :], near_ref[hidden:, :], fars[n - 1][last:, :]))
    oh_ref[...] = new.astype(F32).T[:, :classes].astype(BF16)


def mean_kernel(bounds, *refs):
    n = len(bounds) - 1
    o_ref = refs[3 * n]
    width = 128
    for i in range(n):

        def block(j, carry, i=i):
            s = pl.ds(pl.multiple_of(j * width, width), width)
            at = pl.ds(pl.multiple_of(bounds[i] + j * width, width), width)
            total = refs[i][s, :].astype(F32) + refs[n + i][s, :].astype(F32)
            o_ref[at, :] = ((total + refs[2 * n + i][s, :].astype(F32)) / 3.0).astype(BF16)
            return carry

        lax.fori_loop(0, (bounds[i + 1] - bounds[i]) // width, block, 0)


def tp_move(value, by_x, by_y):
    pairs = [(x * 4 + y, (x + by_x) % 2 * 4 + (y + by_y) % 4) for x in range(2) for y in range(4)]
    return lax.ppermute(value, "tp", pairs)


def rep_move(value, by):
    return lax.ppermute(value, "rep", [(i, (i + by) % 32) for i in range(32)])


def along_y(part):
    up, down, over = tp_move(part, 0, 1), tp_move(part, 0, -1), tp_move(part, 0, 2)
    return call(add_kernel, jax.ShapeDtypeStruct(part.shape, F32), 4, size=200000)(part, over, up, down)


def between(r):
    return r // 16 * 16 + (r % 16 - 4) % 16


def back_two(value):
    return lax.ppermute(value, "rep", [(r, between(r)) for r in range(32)])


def back_rest(value):
    return lax.ppermute(value, "rep", [(between(r), (r + 8) % 32) for r in range(32)])


def tail(level, sent_a, sent_b, pack, stacked, moved, mass, lr_second, lr_head):
    shape = jax.ShapeDtypeStruct
    tied = lax.optimization_barrier
    near = 1 << level
    hidden = sent_a.shape[1]
    pack_near = rep_move(pack, near)
    near_b = rep_move(sent_b, near)
    if level == 2:
        half_way = back_two(sent_b)
        split = 384
        far_first, far_last = rep_move(moved[2][:split], 4), back_rest(back_two(stacked[split:]))
    near_a = rep_move(sent_a, near)
    near_b, pack_near = tied((near_b, pack_near))
    pack_far = rep_move(pack_near, near)
    far_b = back_rest(half_way) if level == 2 else rep_move(near_b, near)
    near_a, pack_far = tied((near_a, pack_far))
    far_a = rep_move(near_a, near)
    if level == 2:
        bounds = (0, split, hidden + 128)
        fars = [far_first, far_last]
    else:
        bounds = (0, hidden + 128)
        fars = [moved[level + 1]]
    new_second, new_head = call(
        partial(rest_kernel, bounds),
        [shape((hidden, D), BF16), shape((D, 125), BF16)],
        7 + len(fars),
        (0, 1),
        size=15000000,
    )(lr_second, lr_head, pack, pack_near, pack_far, stacked, moved[level], *fars)
    bounds = (0, sent_a.shape[0], D)
    new_first = call(partial(mean_kernel, bounds), shape((D, hidden), BF16), 6, size=2000000)(
        sent_a, sent_b, near_a, near_b, far_a, far_b
    )
    new_mass = (mass + pack_near[0, -1:] + pack_far[0, -1:]) / 3.0
    return new_first, new_second, new_head, new_mass


def local(
    images,
    labels,
    first_weight,
    second_weight,
    head_weight,
    push_weights,
    round_index,
    lr_first,
    lr_second,
    lr_head,
):
    hidden = first_weight.shape[1]
    classes = head_weight.shape[1]
    t = lax.axis_index("tp")
    tx, ty = t // 4, t % 4
    shape = jax.ShapeDtypeStruct
    tied = lax.optimization_barrier
    half = SEQ // 2

    own, tok = call(
        norm_kernel, [shape((SEQ, D), BF16), shape((1, D), F32)], 1, size=4000000
    )(images)
    stacked = call(stack_kernel, shape((hidden + 128, D), BF16), 2, size=3000000)(
        second_weight, head_weight
    )
    across = tp_move(own, 1, 0)
    up, down = tp_move(own, 0, 1), tp_move(own, 0, -1)

    def scaled(w):
        return call(scale_kernel, shape(w.shape, BF16), 2, (0,), size=3000000)(push_weights, w)

    order = jnp.stack([(tx + j // 4) % 2 * 4 + (ty + j % 4) % 4 for j in range(8)]).astype(jnp.int32)
    layout, blocks, slopes = [], [], []
    sums = [jnp.zeros((IMG, hidden), F32)]

    def forward(block, pieces):
        rows = sum(p[1] for p in pieces)
        act, slope = pl.pallas_call(
            partial(forward_kernel, pieces),
            out_shape=[shape((IMG, hidden), F32), shape((rows, hidden), F32)],
            in_specs=[SMEM, VMEM, VMEM, VMEM],
            out_specs=[VMEM, ANY],
            scratch_shapes=[
                pltpu.VMEM((max(p[1] for p in pieces), hidden), F32),
                pltpu.VMEM((rows, hidden), F32),
                pltpu.SemaphoreType.DMA((rows // 128,)),
            ],
            compiler_params=PARAMS,
            cost_estimate=pl.CostEstimate(flops=0, bytes_accessed=2500000, transcendentals=0),
        )(order, block, z_first, *sums)
        sums[:] = [act]
        layout.append(pieces)
        blocks.append(block)
        slopes.append(slope)

    z_first, z_second, z_head = scaled(first_weight), scaled(second_weight), scaled(head_weight)
    class_ids = t * classes + jnp.arange(classes, dtype=jnp.int32)
    onehot = (labels[:, None] == class_ids[None, :]).astype(F32)
    hot = lax.dot_general(
        onehot.astype(BF16), z_head, (((1,), (1,)), ((), ())), preferred_element_type=F32
    )
    forward(own, ((0, SEQ, 0),))
    across, up, down, z_second, hot, stacked, *sums = tied(
        (across, up, down, z_second, hot, stacked, *sums)
    )
    up_b, down_b = gathered(
        (((0, 0, SEQ), (1, 0, half)), ((0, 0, SEQ), (2, half, half))), across, up, down
    )
    up_b, down_b = tp_move(up_b, 0, 1), tp_move(down_b, 0, -1)
    by_1 = rep_move(stacked, 1)
    forward(across, ((0, SEQ, 4),))
    forward(up, ((0, SEQ, 3),))
    forward(down, ((0, SEQ, 1),))
    up_b, down_b, by_1, *sums = tied((up_b, down_b, by_1, *sums))
    over_c, over_d = gathered((((0, 0, half),), ((1, half, half),)), up_b, down_b)
    over_c, over_d = tp_move(over_c, 0, 1), tp_move(over_d, 0, -1)
    by_2 = rep_move(by_1, 1)
    forward(up_b, ((0, SEQ, 7), (SEQ, half, 2)))
    forward(down_b, ((0, SEQ, 5), (SEQ, half, 2)))
    over_c, over_d, *sums = tied((over_c, over_d, *sums))
    forward(over_c, ((0, half, 6),))
    forward(over_d, ((0, half, 6),))

    mean_act, part = call(
        pool_kernel,
        [shape((IMG, hidden), F32), shape((IMG, 2 * D), F32)],
        5,
        (0,),
        size=3000000,
    )(order, sums[0], z_second, tok, hot)
    part, by_2 = tied((part, by_2))
    part = call(pair_kernel, shape(part.shape, F32), 2, size=200000)(part, tp_move(part, 1, 0))
    part, by_2 = tied((part, by_2))
    by_4 = rep_move(by_2, 2)
    up, down, over = tp_move(part, 0, 1), tp_move(part, 0, -1), tp_move(part, 0, 2)
    pooled, hot, expo, part = call(
        logit_kernel,
        [shape((IMG, D), F32), shape((IMG, D), F32), shape((IMG, classes), F32), shape((IMG, D + 128), F32)],
        5,
        size=3000000,
    )(part, over, up, down, z_head)
    part = along_y(part)
    mass = push_weights.astype(BF16).astype(F32)
    dmean, pack = call(
        grad_kernel,
        [shape((IMG, hidden), F32), shape((IMG, hidden + 2 * D + 128), F32)],
        9,
        (8,),
        size=3000000,
    )(part, tp_move(part, 1, 0), hot, onehot, expo, z_second, mean_act, pooled, mass)

    n = len(blocks)
    dpres = pl.pallas_call(
        partial(dpre_kernel, layout),
        out_shape=[shape(g.shape, BF16) for g in slopes],
        in_specs=[SMEM] + [ANY] * n + [VMEM],
        out_specs=[VMEM] * n,
        scratch_shapes=[pltpu.VMEM((IMG * SEQ, hidden), F32), pltpu.SemaphoreType.DMA((n,))],
        compiler_params=PARAMS,
        cost_estimate=pl.CostEstimate(flops=0, bytes_accessed=6000000, transcendentals=0),
    )(order, *slopes, dmean)

    def sent_rows(begin, end):
        return call(
            partial(first_kernel, layout, begin),
            shape((end - begin, hidden), BF16),
            2 + 2 * n,
            (0,),
            size=6000000,
        )(lr_first, *blocks, *dpres, first_weight)

    cut = 384
    return lax.switch(
        jnp.clip(round_index[0], 0, 2),
        [partial(tail, level) for level in range(3)],
        sent_rows(0, cut),
        sent_rows(cut, D),
        pack,
        stacked,
        (by_1, by_2, by_4),
        mass,
        lr_second,
        lr_head,
    )


def solution(mesh):
    return jax.shard_map(
        local,
        mesh=mesh,
        in_specs=(
            P(("rep", "tp"), None),
            P("rep"),
            P("rep", "tp"),
            P(("rep", "tp"), None),
            P("rep", "tp"),
            P("rep"),
            P(),
            P(),
            P(),
            P(),
        ),
        out_specs=(P("rep", "tp"), P(("rep", "tp"), None), P("rep", "tp"), P("rep")),
        check_vma=False,
    )
```

```python
from functools import partial

import jax
import jax.numpy as jnp
from jax import lax
from jax.experimental import pallas as pl
from jax.experimental.pallas import tpu as pltpu
from jax.sharding import PartitionSpec as P

SEQ = 256
IMG = 8
D = 1024

COEF = 0.7978845608
CUBIC = 0.044715
F32 = jnp.float32
BF16 = jnp.bfloat16

VMEM = pl.BlockSpec(memory_space=pltpu.VMEM)
SMEM = pl.BlockSpec(memory_space=pltpu.SMEM)
ANY = pl.BlockSpec(memory_space=pl.ANY)
PARAMS = pltpu.CompilerParams(vmem_limit_bytes=10 * 1024 * 1024)


def call(body, out_shapes, n_in, scalars=(), scratch=(), flops=0, size=0):
    specs = [SMEM if i in scalars else VMEM for i in range(n_in)]
    single = not isinstance(out_shapes, (list, tuple))
    return pl.pallas_call(
        body,
        out_shape=out_shapes,
        in_specs=specs,
        out_specs=VMEM if single else [VMEM] * len(out_shapes),
        scratch_shapes=list(scratch),
        compiler_params=PARAMS,
        cost_estimate=pl.CostEstimate(flops=flops, bytes_accessed=size, transcendentals=0),
    )


def split3(v):
    a = v.astype(BF16)
    r = v - a.astype(F32)
    b = r.astype(BF16)
    c = (r - b.astype(F32)).astype(BF16)
    return a, b, c


def dot(a, b, dims):
    return lax.dot_general(a, b, (dims, ((), ())), preferred_element_type=F32)


def exact_right(a, b, dims):
    n = a.shape[0]
    p = dot(jnp.concatenate(split3(a), axis=0), b, dims)
    return p[:n] + p[n : 2 * n] + p[2 * n : 3 * n]


def outer(a, b):
    a1, a2, a3 = split3(a)
    b1, b2, b3 = split3(b)
    left = jnp.concatenate([a1, a1, a1, a2, a2, a3], axis=0)
    right = jnp.concatenate([b1, b2, b3, b1, b2, b1], axis=0)
    return dot(left, right, ((0,), (0,)))


def norm_kernel(x_ref, o_ref, m_ref):
    rows = x_ref.shape[0]
    step = 64

    def slab(i, total):
        at = pl.ds(pl.multiple_of(i * step, step), step)
        v = x_ref[at, :].astype(F32)
        center = v - jnp.mean(v, axis=-1, keepdims=True)
        spread = jnp.mean(center * center, axis=-1, keepdims=True)
        o_ref[at, :] = (center * lax.rsqrt(spread + 1e-05)).astype(BF16)
        return total + jnp.sum(v, axis=0, keepdims=True)

    total = lax.fori_loop(0, rows // step, slab, jnp.zeros((1, D), F32))
    m_ref[...] = total / SEQ


def stack_kernel(second_ref, head_ref, o_ref):
    rows = second_ref.shape[0]
    o_ref[:rows, :] = second_ref[...]
    classes = head_ref.shape[1]
    width = 256
    for at in range(0, D, width):
        part = head_ref[at : at + width, :].astype(F32)
        part = jnp.concatenate([part, jnp.zeros((width, 128 - classes), F32)], axis=1)
        o_ref[rows:, at : at + width] = part.T.astype(BF16)


def gather_kernel(picks, n, *refs):
    for pick, o_ref in zip(picks, refs[n:]):
        to = 0
        for which, begin, rows in pick:
            o_ref[to : to + rows, :] = refs[which][begin : begin + rows, :]
            to += rows


def gathered(picks, *arrays):
    shapes = [jax.ShapeDtypeStruct((sum(p[2] for p in pick), arrays[0].shape[1]), BF16) for pick in picks]
    return call(partial(gather_kernel, picks, len(arrays)), shapes, len(arrays), size=2000000)(*arrays)


def scale_kernel(mass_ref, w_ref, o_ref):
    step = 128

    def slab(i, carry):
        at = pl.ds(pl.multiple_of(i * step, step), step)
        o_ref[at, :] = (w_ref[at, :].astype(F32) / mass_ref[0]).astype(BF16)
        return carry

    lax.fori_loop(0, w_ref.shape[0] // step, slab, 0)


def rows_of(index, rows, width):
    at = lax.broadcasted_iota(jnp.int32, (IMG, width), 0)
    return jnp.where(at == index, jnp.broadcast_to(rows, (IMG, width)), 0.0)


def forward_kernel(
    pieces, order_ref, x_ref, z_ref, act_in, act_ref, slope_out, pre_ref, slope_ref, sems
):
    step = 32
    part = 128
    width = z_ref.shape[1]
    act_sum = act_in[...]
    copies = []
    to = 0
    for begin, rows, slot in pieces:
        pre_ref[:rows, :] = dot(x_ref[begin : begin + rows, :], z_ref[...], ((1,), (0,)))
        total = jnp.zeros((8, width), F32)
        for at in range(0, rows, part):

            def slab(i, total, at=at, to=to):
                pre = pre_ref[pl.ds(pl.multiple_of(at + i * step, step), step), :]
                square = pre * pre
                t = jnp.tanh(COEF * (pre + CUBIC * square * pre))
                act = 0.5 * pre * (1.0 + t)
                slope_ref[pl.ds(pl.multiple_of(to + i * step, step), step), :] = 0.5 * (
                    1.0 + t
                ) + 0.5 * pre * (1.0 - t * t) * COEF * (1.0 + 3.0 * CUBIC * square)
                return total + jnp.sum(act.reshape(step // 8, 8, width), axis=0)

            total = lax.fori_loop(0, part // step, slab, total)
            where = pl.ds(to, part)
            copies.append(
                pltpu.make_async_copy(slope_ref.at[where], slope_out.at[where], sems.at[to // part])
            )
            copies[-1].start()
            to += part
        act_sum = act_sum + rows_of(order_ref[slot], jnp.sum(total, axis=0, keepdims=True), width)
    act_ref[...] = act_sum
    for copy in copies:
        copy.wait()


def pool_kernel(order_ref, sum_ref, z_ref, tok_ref, hot_ref, act_ref, out_ref):
    mean_act = sum_ref[...] / SEQ
    act_ref[...] = mean_act
    part = exact_right(mean_act, z_ref[...], ((1,), (0,))) + rows_of(order_ref[0], tok_ref[...], D)
    out_ref[:, :D] = part
    out_ref[:, D:] = hot_ref[...]


def add_kernel(own_ref, over_ref, up_ref, down_ref, o_ref):
    o_ref[...] = (own_ref[...] + over_ref[...]) + (up_ref[...] + down_ref[...])


def pair_kernel(one_ref, two_ref, o_ref):
    o_ref[...] = one_ref[...] + two_ref[...]


def logit_kernel(own_ref, over_ref, up_ref, down_ref, zh_ref, pooled_ref, hot_ref, expo_ref, out_ref):
    both = (own_ref[...] + over_ref[...]) + (up_ref[...] + down_ref[...])
    pooled = both[:, :D]
    hot_ref[...] = both[:, D:]
    pooled_b = pooled.astype(BF16)
    pooled_ref[...] = pooled_b.astype(F32)
    zh = zh_ref[...]
    expo = jnp.exp(dot(pooled_b, zh, ((1,), (0,))))
    expo_ref[...] = expo
    part = exact_right(expo, zh, ((1,), (1,)))
    total = jnp.broadcast_to(jnp.sum(expo, axis=1, keepdims=True), (IMG, 128))
    out_ref[:, :D] = part
    out_ref[:, D:] = total


def grad_kernel(one_ref, two_ref, hot_ref, own_hot_ref, expo_ref, z_ref, act_ref, pooled_ref, mass_ref, dmean_ref, pack_ref):
    both = one_ref[...] + two_ref[...]
    total = both[:, D : D + 1]
    dpool = (both[:, :D] / total - hot_ref[...]) / IMG
    dlog = (expo_ref[...] / total - own_hot_ref[...]) / IMG
    dmean_ref[...] = exact_right(dpool, z_ref[...], ((1,), (1,)))
    hidden = z_ref.shape[0]
    classes = dlog.shape[1]
    pack_ref[:, :hidden] = act_ref[...]
    pack_ref[:, hidden : hidden + D] = dpool
    pack_ref[:, hidden + D : hidden + 2 * D] = pooled_ref[...]
    pack_ref[:, hidden + 2 * D :] = jnp.full((IMG, 128), mass_ref[0], F32)
    pack_ref[:, hidden + 2 * D : hidden + 2 * D + classes] = dlog


def dpre_kernel(layout, order_ref, *refs):
    n = len(layout)
    slopes, dmean_ref, outs = refs[:n], refs[n], refs[n + 1 : 2 * n + 1]
    held, sems = refs[2 * n + 1 :]
    copies = []
    to = 0
    for i, ref in enumerate(slopes):
        copies.append(pltpu.make_async_copy(ref, held.at[pl.ds(to, ref.shape[0])], sems.at[i]))
        copies[-1].start()
        to += ref.shape[0]
    dmean = dmean_ref[...] / SEQ
    hidden = dmean.shape[1]
    step = 32
    base = 0
    for pieces, copy, dpre_ref in zip(layout, copies, outs):
        copy.wait()
        to = 0
        for _, rows, slot in pieces:
            at = lax.broadcasted_iota(jnp.int32, (IMG, hidden), 0)
            row = jnp.sum(jnp.where(at == order_ref[slot], dmean, 0.0), axis=0, keepdims=True)

            def slab(i, carry, to=to, base=base, row=row, dpre_ref=dpre_ref):
                at = pl.multiple_of(i * step, step)
                dpre_ref[pl.ds(to + at, step), :] = (row * held[pl.ds(base + to + at, step), :]).astype(BF16)
                return carry

            lax.fori_loop(0, rows // step, slab, 0)
            to += rows
        base += to


def first_kernel(layout, begin, lr_ref, *refs):
    n = len(layout)
    xs, dpre_refs = refs[:n], refs[n : 2 * n]
    w_ref, o_ref = refs[2 * n :]
    hidden = o_ref.shape[1]
    width = 128
    for lo in range(0, o_ref.shape[0], width):
        at = begin + lo
        grad = jnp.zeros((width, hidden), F32)
        for pieces, x_ref, dpre_ref in zip(layout, xs, dpre_refs):
            to = 0
            for row, rows, _ in pieces:
                grad = grad + dot(
                    x_ref[row : row + rows, at : at + width], dpre_ref[to : to + rows, :], ((0,), (0,))
                )
                to += rows
        o_ref[lo : lo + width, :] = (
            w_ref[at : at + width, :].astype(F32) - lr_ref[0] * grad
        ).astype(BF16)


def rest_kernel(bounds, lr2_ref, lrh_ref, *refs):
    n = len(bounds) - 1
    packs, own_ref, near_ref, fars = refs[0:3], refs[3], refs[4], refs[5 : 5 + n]
    o2_ref, oh_ref = refs[5 + n :]
    hidden = o2_ref.shape[0]
    classes = oh_ref.shape[1]
    width = 128

    def mean(rate, grads, weights):
        total = None
        for grad, w in zip(grads, weights):
            sent = (w.astype(F32) - rate * grad).astype(BF16).astype(F32)
            total = sent if total is None else total + sent
        return (total / 3.0).astype(BF16)

    for i in range(n):

        def block(j, carry, i=i):
            lo = pl.ds(pl.multiple_of(j * width, width), width)
            at = pl.ds(pl.multiple_of(bounds[i] + j * width, width), width)
            grads = [outer(pack[:, at], pack[:, hidden : hidden + D]) for pack in packs]
            o2_ref[at, :] = mean(lr2_ref[0], grads, (own_ref[at, :], near_ref[at, :], fars[i][lo, :]))
            return carry

        lax.fori_loop(0, (min(bounds[i + 1], hidden) - bounds[i]) // width, block, 0)
    grads = []
    for pack in packs:
        left = jnp.concatenate(split3(pack[:, hidden + 2 * D :]), axis=0)
        right = pack[:, hidden + D : hidden + 2 * D].astype(BF16)
        grads.append(dot(left, jnp.concatenate([right] * 3, axis=0), ((0,), (0,))))
    last = fars[n - 1].shape[0] - width
    new = mean(lrh_ref[0], grads, (own_ref[hidden:, :], near_ref[hidden:, :], fars[n - 1][last:, :]))
    oh_ref[...] = new.astype(F32).T[:, :classes].astype(BF16)


def mean_kernel(bounds, *refs):
    n = len(bounds) - 1
    o_ref = refs[3 * n]
    width = 128
    for i in range(n):

        def block(j, carry, i=i):
            s = pl.ds(pl.multiple_of(j * width, width), width)
            at = pl.ds(pl.multiple_of(bounds[i] + j * width, width), width)
            total = refs[i][s, :].astype(F32) + refs[n + i][s, :].astype(F32)
            o_ref[at, :] = ((total + refs[2 * n + i][s, :].astype(F32)) / 3.0).astype(BF16)
            return carry

        lax.fori_loop(0, (bounds[i + 1] - bounds[i]) // width, block, 0)


def tp_move(value, by_x, by_y):
    pairs = [(x * 4 + y, (x + by_x) % 2 * 4 + (y + by_y) % 4) for x in range(2) for y in range(4)]
    return lax.ppermute(value, "tp", pairs)


def rep_move(value, by):
    return lax.ppermute(value, "rep", [(i, (i + by) % 32) for i in range(32)])


def along_y(part):
    up, down, over = tp_move(part, 0, 1), tp_move(part, 0, -1), tp_move(part, 0, 2)
    return call(add_kernel, jax.ShapeDtypeStruct(part.shape, F32), 4, size=200000)(part, over, up, down)


def between(r):
    return r // 16 * 16 + (r % 16 - 4) % 16


def back_two(value):
    return lax.ppermute(value, "rep", [(r, between(r)) for r in range(32)])


def back_rest(value):
    return lax.ppermute(value, "rep", [(between(r), (r + 8) % 32) for r in range(32)])


def tail(level, sent_a, sent_b, pack, stacked, moved, mass, lr_second, lr_head):
    shape = jax.ShapeDtypeStruct
    tied = lax.optimization_barrier
    near = 1 << level
    hidden = sent_a.shape[1]
    pack_near = rep_move(pack, near)
    near_b = rep_move(sent_b, near)
    if level == 2:
        half_way = back_two(sent_b)
        split = 384
        far_first, far_last = rep_move(moved[2], 4), back_rest(back_two(stacked[split:]))
    near_a = rep_move(sent_a, near)
    near_b, pack_near = tied((near_b, pack_near))
    pack_far = rep_move(pack_near, near)
    far_b = back_rest(half_way) if level == 2 else rep_move(near_b, near)
    near_a, pack_far = tied((near_a, pack_far))
    far_a = rep_move(near_a, near)
    if level == 2:
        bounds = (0, split, hidden + 128)
        fars = [far_first, far_last]
        weight_near = jnp.concatenate([moved[2], moved[3]])
    elif level == 1:
        bounds = (0, moved[2].shape[0], hidden + 128)
        fars = [moved[2], moved[3]]
        weight_near = moved[1]
    else:
        bounds = (0, hidden + 128)
        fars = [moved[1]]
        weight_near = moved[0]
    new_second, new_head = call(
        partial(rest_kernel, bounds),
        [shape((hidden, D), BF16), shape((D, 125), BF16)],
        7 + len(fars),
        (0, 1),
        size=15000000,
    )(lr_second, lr_head, pack, pack_near, pack_far, stacked, weight_near, *fars)
    bounds = (0, sent_a.shape[0], D)
    new_first = call(partial(mean_kernel, bounds), shape((D, hidden), BF16), 6, size=2000000)(
        sent_a, sent_b, near_a, near_b, far_a, far_b
    )
    new_mass = (mass + pack_near[0, -1:] + pack_far[0, -1:]) / 3.0
    return new_first, new_second, new_head, new_mass


def local(
    images,
    labels,
    first_weight,
    second_weight,
    head_weight,
    push_weights,
    round_index,
    lr_first,
    lr_second,
    lr_head,
):
    hidden = first_weight.shape[1]
    classes = head_weight.shape[1]
    t = lax.axis_index("tp")
    tx, ty = t // 4, t % 4
    shape = jax.ShapeDtypeStruct
    tied = lax.optimization_barrier
    half = SEQ // 2

    own, tok = call(
        norm_kernel, [shape((SEQ, D), BF16), shape((1, D), F32)], 1, size=4000000
    )(images)
    stacked = call(stack_kernel, shape((hidden + 128, D), BF16), 2, size=3000000)(
        second_weight, head_weight
    )
    across = tp_move(own, 1, 0)
    up, down = tp_move(own, 0, 1), tp_move(own, 0, -1)

    def scaled(w):
        return call(scale_kernel, shape(w.shape, BF16), 2, (0,), size=3000000)(push_weights, w)

    order = jnp.stack([(tx + j // 4) % 2 * 4 + (ty + j % 4) % 4 for j in range(8)]).astype(jnp.int32)
    layout, blocks, slopes = [], [], []
    sums = [jnp.zeros((IMG, hidden), F32)]

    def forward(block, pieces):
        rows = sum(p[1] for p in pieces)
        act, slope = pl.pallas_call(
            partial(forward_kernel, pieces),
            out_shape=[shape((IMG, hidden), F32), shape((rows, hidden), F32)],
            in_specs=[SMEM, VMEM, VMEM, VMEM],
            out_specs=[VMEM, ANY],
            scratch_shapes=[
                pltpu.VMEM((max(p[1] for p in pieces), hidden), F32),
                pltpu.VMEM((rows, hidden), F32),
                pltpu.SemaphoreType.DMA((rows // 128,)),
            ],
            compiler_params=PARAMS,
            cost_estimate=pl.CostEstimate(flops=0, bytes_accessed=2500000, transcendentals=0),
        )(order, block, z_first, *sums)
        sums[:] = [act]
        layout.append(pieces)
        blocks.append(block)
        slopes.append(slope)

    z_first, z_second, z_head = scaled(first_weight), scaled(second_weight), scaled(head_weight)
    class_ids = t * classes + jnp.arange(classes, dtype=jnp.int32)
    onehot = (labels[:, None] == class_ids[None, :]).astype(F32)
    hot = lax.dot_general(
        onehot.astype(BF16), z_head, (((1,), (1,)), ((), ())), preferred_element_type=F32
    )
    forward(own, ((0, SEQ, 0),))
    across, up, down, z_second, hot, stacked, *sums = tied(
        (across, up, down, z_second, hot, stacked, *sums)
    )
    up_b, down_b = gathered(
        (((0, 0, SEQ), (1, 0, half)), ((0, 0, SEQ), (2, half, half))), across, up, down
    )
    up_b, down_b = tp_move(up_b, 0, 1), tp_move(down_b, 0, -1)
    by_1 = rep_move(stacked, 1)
    forward(across, ((0, SEQ, 4),))
    forward(up, ((0, SEQ, 3),))
    forward(down, ((0, SEQ, 1),))
    up_b, down_b, by_1, *sums = tied((up_b, down_b, by_1, *sums))
    over_c, over_d = gathered((((0, 0, half),), ((1, half, half),)), up_b, down_b)
    over_c, over_d = tp_move(over_c, 0, 1), tp_move(over_d, 0, -1)
    by_2 = rep_move(by_1, 1)
    forward(up_b, ((0, SEQ, 7), (SEQ, half, 2)))
    forward(down_b, ((0, SEQ, 5), (SEQ, half, 2)))
    over_c, over_d, *sums = tied((over_c, over_d, *sums))
    forward(over_c, ((0, half, 6),))
    forward(over_d, ((0, half, 6),))

    mean_act, part = call(
        pool_kernel,
        [shape((IMG, hidden), F32), shape((IMG, 2 * D), F32)],
        5,
        (0,),
        size=3000000,
    )(order, sums[0], z_second, tok, hot)
    part = call(pair_kernel, shape(part.shape, F32), 2, size=200000)(part, tp_move(part, 1, 0))
    part, by_2 = tied((part, by_2))
    upper, lower = gathered((((0, 0, 384),), ((0, 384, hidden + 128 - 384),)), by_2)
    upper = rep_move(upper, 2)
    up, down, over = tp_move(part, 0, 1), tp_move(part, 0, -1), tp_move(part, 0, 2)
    pooled, hot, expo, part = call(
        logit_kernel,
        [shape((IMG, D), F32), shape((IMG, D), F32), shape((IMG, classes), F32), shape((IMG, D + 128), F32)],
        5,
        size=3000000,
    )(part, over, up, down, z_head)
    part, upper = tied((along_y(part), upper))
    over_x, lower = tied((tp_move(part, 1, 0), lower))
    lower = rep_move(lower, 2)
    mass = push_weights.astype(BF16).astype(F32)
    dmean, pack = call(
        grad_kernel,
        [shape((IMG, hidden), F32), shape((IMG, hidden + 2 * D + 128), F32)],
        9,
        (8,),
        size=3000000,
    )(part, over_x, hot, onehot, expo, z_second, mean_act, pooled, mass)

    n = len(blocks)
    dpres = pl.pallas_call(
        partial(dpre_kernel, layout),
        out_shape=[shape(g.shape, BF16) for g in slopes],
        in_specs=[SMEM] + [ANY] * n + [VMEM],
        out_specs=[VMEM] * n,
        scratch_shapes=[pltpu.VMEM((IMG * SEQ, hidden), F32), pltpu.SemaphoreType.DMA((n,))],
        compiler_params=PARAMS,
        cost_estimate=pl.CostEstimate(flops=0, bytes_accessed=6000000, transcendentals=0),
    )(order, *slopes, dmean)

    def sent_rows(begin, end):
        return call(
            partial(first_kernel, layout, begin),
            shape((end - begin, hidden), BF16),
            2 + 2 * n,
            (0,),
            size=6000000,
        )(lr_first, *blocks, *dpres, first_weight)

    cut = 384
    return lax.switch(
        jnp.clip(round_index[0], 0, 2),
        [partial(tail, level) for level in range(3)],
        sent_rows(0, cut),
        sent_rows(cut, D),
        pack,
        stacked,
        (by_1, by_2, upper, lower),
        mass,
        lr_second,
        lr_head,
    )


def solution(mesh):
    return jax.shard_map(
        local,
        mesh=mesh,
        in_specs=(
            P(("rep", "tp"), None),
            P("rep"),
            P("rep", "tp"),
            P(("rep", "tp"), None),
            P("rep", "tp"),
            P("rep"),
            P(),
            P(),
            P(),
            P(),
        ),
        out_specs=(P("rep", "tp"), P(("rep", "tp"), None), P("rep", "tp"), P("rep")),
        check_vma=False,
    )
```
